512 devices in a mesh: dp: 4 (over z_hi), fsdp: 8 (over x, core), tensor: 16 (over z_lo, y).
Axes of the slice: x: 4, y: 4, z: 16 (z_hi: 4, z_lo: 4; z = z_hi * 4 + z_lo), core: 2. Of those that a mesh axis runs over, the one named last changes fastest.
Arguments:
- features: bfloat16 [8192, 8192], P(('dp', 'fsdp'), 'tensor'), may hold values from -6 to 6
- cotangent: bfloat16 [8192, 32768], P(('dp', 'fsdp'), 'tensor'), may hold values from -6 to 6
- butterfly: bfloat16 [8, 128, 64, 256], P(None, 'tensor', 'fsdp'), may hold values from -0.25 to 0.25
- left_factor: bfloat16 [8192, 256], P('tensor', 'fsdp'), may hold values from -0.0625 to 0.0625
- right_factor: bfloat16 [256, 32768], P('fsdp', 'tensor'), may hold values from -0.375 to 0.375
Outputs:
- activation: bfloat16 [8192, 32768], P(('dp', 'fsdp'), 'tensor')
- feature_grad: bfloat16 [8192, 8192], P(('dp', 'fsdp'), 'tensor')
- butterfly_grad: float32 [8, 128, 64, 256], P(None, 'tensor', 'fsdp')
- left_grad: float32 [8192, 256], P('tensor', 'fsdp')
- right_grad: float32 [256, 32768], P('fsdp', 'tensor')
The draws below stay inside these ranges and needn't reach their ends.
All inputs are finite; a program needn't handle non-finite values.
Results may differ from the reference program's by a relative error of at most 0.017.
Values may be sent and summed in bfloat16 or wider, within the bound.
A program may use at most 64 MiB of HBM per device.

```python
import jax
import jax.numpy as jnp
from jax import lax

D = 8192
FF = 32768
R = 256
B = 64
BITS = 7
TOK_DEV = 256
TOKENS = 8192
GROUPS = 128
HG = 256
TERMS = 8
N_DP = 4
N_FSDP = 8
N_TENSOR = 16


def levels(key, extent, split, smallest, top_value):
    def one(position, parts):
        steps = jax.random.uniform(jax.random.fold_in(jax.random.fold_in(key, 6), position), (parts,), jnp.float32, smallest / len(split), top_value / len(split))
        return jnp.repeat(jnp.exp(steps), extent[position] // parts).reshape((-1,) + (1,) * (len(extent) - position - 1))

    gain = one(*split[0])
    for cut in split[1:]:
        gain = gain * one(*cut)
    return gain


def gaussian(key, extent, spread, reach, shards=(), kind=jnp.bfloat16):
    result = jax.random.normal(key, extent, jnp.float32) * spread
    if len(shards) > 0:
        result = levels(key, extent, shards, -0.22, 0.18) * result
    return jnp.clip(result, min=-reach, max=reach).astype(kind)


def setup_inputs(seed: int = 0) -> dict:
    keys = jax.random.split(jax.random.key(seed), 6)
    features = gaussian(keys[0], (TOKENS, D), 1.0, 6.0, ((0, 32), (1, 16)))
    cotangent = gaussian(keys[1], (TOKENS, FF), 1.0, 6.0, ((0, 32), (1, 16)))
    butterfly = gaussian(keys[2], (TERMS, GROUPS, B, HG), (TERMS * B) ** -0.5, 0.25, ((1, 16), (2, 8)))
    left_factor = gaussian(keys[3], (D, R), D ** -0.5, 0.0625, ((0, 16), (1, 8)))
    right_factor = gaussian(keys[4], (R, FF), R ** -0.5, 0.375, ((0, 8), (1, 16)))
    return dict(features=features, cotangent=cotangent, butterfly=butterfly, left_factor=left_factor, right_factor=right_factor)


def reference(features, cotangent, butterfly, left_factor, right_factor):
    blocks = N_DP * N_FSDP
    local_bits = (GROUPS // N_TENSOR).bit_length() - 1
    feat_blocks = features.reshape(blocks, TOK_DEV, D)
    cot_blocks = cotangent.reshape(blocks, TOK_DEV, FF)
    weight_full = butterfly.astype(jnp.float32)
    base = jnp.arange(GROUPS, dtype=jnp.int32)
    perms = [base] + [jnp.bitwise_xor(base, 1 << level) for level in range(BITS)]

    def block_step(carry, pieces):
        grad_bfly, grad_left, grad_right = carry
        feat_rows, cot_rows = pieces
        grouped = feat_rows.astype(jnp.float32).reshape(TOK_DEV, GROUPS, B)
        partners = [grouped[:, perm] for perm in perms]
        pre = jnp.zeros((TOK_DEV, GROUPS, HG), jnp.float32)
        for term_idx in range(TERMS):
            pre = pre + jnp.einsum('ngb,gbh->ngh', partners[term_idx], weight_full[term_idx])
        lowrank = jnp.dot(feat_rows, left_factor, preferred_element_type=jnp.float32).astype(jnp.bfloat16)
        pre = pre.reshape(TOK_DEV, FF) + jnp.dot(lowrank, right_factor, preferred_element_type=jnp.float32)
        act, pull = jax.vjp(jax.nn.gelu, pre)
        gpre = pull(cot_rows.astype(jnp.float32))[0].astype(jnp.bfloat16)
        gpre_full = gpre.astype(jnp.float32).reshape(TOK_DEV, GROUPS, HG)
        part_bfly = jnp.stack([jnp.einsum('ngb,ngh->gbh', partners[term_idx], gpre_full) for term_idx in range(TERMS)])
        part_bfly = lax.optimization_barrier(part_bfly.astype(jnp.bfloat16)).astype(jnp.float32)
        glow = jnp.dot(gpre, right_factor.T, preferred_element_type=jnp.float32).astype(jnp.bfloat16)
        part_left = lax.optimization_barrier(jnp.dot(feat_rows.T, glow, preferred_element_type=jnp.float32).astype(jnp.bfloat16)).astype(jnp.float32)
        part_right = lax.optimization_barrier(jnp.dot(lowrank.T, gpre, preferred_element_type=jnp.float32).astype(jnp.bfloat16)).astype(jnp.float32)
        dfeat = jnp.dot(glow, left_factor.T, preferred_element_type=jnp.float32)
        for term_idx in range(TERMS):
            perm = perms[term_idx]
            term = jnp.einsum('ngh,gbh->ngb', gpre_full[:, perm], weight_full[term_idx][perm])
            if term_idx >= 1 and term_idx - 1 >= local_bits:
                term = lax.optimization_barrier(term.astype(jnp.bfloat16)).astype(jnp.float32)
            dfeat = dfeat + term.reshape(TOK_DEV, D)
        carry = (grad_bfly + part_bfly, grad_left + part_left, grad_right + part_right)
        return (carry, (act.astype(jnp.bfloat16), dfeat.astype(jnp.bfloat16)))
    init = (jnp.zeros((TERMS, GROUPS, B, HG), jnp.float32), jnp.zeros((D, R), jnp.float32), jnp.zeros((R, FF), jnp.float32))
    sums, outs = lax.scan(block_step, init, (feat_blocks, cot_blocks))
    activation = outs[0].reshape(TOKENS, FF)
    feature_grad = outs[1].reshape(TOKENS, D)
    return (activation, feature_grad, sums[0], sums[1], sums[2])
```

```python
import jax
import jax.numpy as jnp
from jax import lax
from jax.experimental import pallas as pl
from jax.experimental.pallas import tpu as pltpu
from jax.sharding import PartitionSpec as P

F32, BF16 = jnp.float32, jnp.bfloat16
TOK, PAIRS, LANES = 256, 4, 128
KZ, NH = 1152, 512
ROWS, COLS = 192, 256
LROWS, LCOLS = 32, 512
GELU_A, GELU_B = 0.7978845608028654, 0.044715
NT = (((1,), (1,)), ((), ()))


def rdma(src, dst, send_sem, recv_sem, device):
    return pltpu.make_async_remote_copy(
        src_ref=src,
        dst_ref=dst,
        send_sem=send_sem,
        recv_sem=recv_sem,
        device_id=device,
        device_id_type=pl.DeviceIdType.MESH,
    )


def flip(v, bits):
    if bits == 1:
        return v + 1 - 2 * lax.rem(v, 2)
    if bits == 2:
        return lax.rem(v + 2, 4)
    return 3 - v


class Place:
    def __init__(self):
        dp, fsdp, tensor = lax.axis_index("dp"), lax.axis_index("fsdp"), lax.axis_index("tensor")
        self.z, self.x, self.k = dp, lax.div(fsdp, 2), lax.rem(fsdp, 2)
        zl, y = lax.div(tensor, 4), lax.rem(tensor, 4)
        self.y = y
        self.xright, self.xleft, self.xfar = (lax.rem(self.x + i, 4) for i in (1, 3, 2))
        self.zright, self.zleft, self.zfar = (lax.rem(self.z + i, 4) for i in (1, 3, 2))
        self.sib = (dp, 2 * self.x + 1 - self.k, tensor)
        self.xr = (dp, 2 * self.xright + self.k, tensor)
        self.xl = (dp, 2 * self.xleft + self.k, tensor)
        self.zr = (self.zright, fsdp, tensor)
        self.zl = (self.zleft, fsdp, tensor)
        self.ys = [(dp, fsdp, zl * 4 + flip(y, j)) for j in (1, 2, 3)]
        self.zs = [(dp, fsdp, flip(zl, j) * 4 + y) for j in (1, 2, 3)]
        self.levels = [self.ys[0], self.ys[1], self.zs[0], self.zs[1]]
        self.all = [self.sib, self.xr, self.xl, self.zr, self.zl] + self.ys + self.zs


class Gather:
    def __init__(self, me, src, buf, ss, rs, rows):
        self.me, self.src, self.buf, self.ss, self.rs, self.half = me, src, buf, ss, rs, rows // 2

    def copy(self, i, device):
        me, buf, h = self.me, self.buf, self.half
        src = self.src if i in (0, 1, 4) else None
        ref = {
            0: lambda: buf.at[me.x, me.k],
            1: lambda: buf.at[me.x, me.k],
            2: lambda: buf.at[me.xleft, me.k, pl.ds(0, h)],
            3: lambda: buf.at[me.xright, me.k, pl.ds(h, h)],
            4: lambda: buf.at[me.x, me.k],
            5: lambda: buf.at[me.xleft, me.k],
            6: lambda: buf.at[me.xright, me.k],
            7: lambda: buf.at[me.xfar, me.k],
        }[i]()
        return rdma(ref if src is None else src, ref, self.ss.at[i], self.rs.at[i], device)

    def first(self):
        me = self.me
        self.copy(0, me.xr).start()
        self.copy(1, me.xl).start()
        self.copy(4, me.sib).start()

    def second(self):
        me = self.me
        self.wait(0)
        self.copy(2, me.xr).start()
        self.copy(5, me.sib).start()
        self.wait(1)
        self.copy(3, me.xl).start()
        self.copy(6, me.sib).start()

    def third(self):
        self.wait(2)
        self.wait(3)
        self.copy(7, self.me.sib).start()

    def last(self):
        for i in (4, 5, 6, 7):
            self.wait(i)

    def wait(self, i):
        self.copy(i, self.me.sib).wait_recv()

    def wait_sends(self):
        for i in range(8):
            self.copy(i, self.me.sib).wait_send()


def add(*parts):
    total = parts[0].astype(F32)
    for part in parts[1:]:
        total = total + part.astype(F32)
    return total


class Reduce:
    def __init__(self, me, bufs, ss, rs, half, split):
        self.me, self.ss, self.rs, self.half, self.split = me, ss, rs, half, split
        self.part, self.fromsib, self.sums, self.h1, self.h2, self.b, self.z1, self.z2, self.g = bufs

    def ends(self, i):
        me, h = self.me, self.half
        return {
            0: lambda: (self.part.at[1 - me.k], self.fromsib, me.sib),
            1: lambda: (self.sums.at[me.xfar, pl.ds(0, h)], self.h1.at[0], me.xr),
            2: lambda: (self.sums.at[me.xfar, pl.ds(h, h)], self.h1.at[1], me.xl),
            3: lambda: (self.sums.at[me.xright], self.h2.at[0], me.xr),
            4: lambda: (self.sums.at[me.xleft], self.h2.at[1], me.xl),
            5: lambda: (self.b.at[me.zfar, 0], self.z1.at[0], me.zr),
            6: lambda: (self.b.at[me.zfar, 1], self.z1.at[1], me.zl),
            7: lambda: (self.b.at[me.zright], self.z2.at[0], me.zr),
            8: lambda: (self.b.at[me.zleft], self.z2.at[1], me.zl),
            9: lambda: (self.g.at[me.z], self.g.at[me.z], me.zr),
            10: lambda: (self.g.at[me.z], self.g.at[me.z], me.zl),
            11: lambda: (self.g.at[me.zleft, 0], self.g.at[me.zleft, 0], me.zr),
            12: lambda: (self.g.at[me.zright, 1], self.g.at[me.zright, 1], me.zl),
        }[i]()

    def send(self, i):
        src, dst, device = self.ends(i)
        rdma(src, dst, self.ss.at[i], self.rs.at[i], device).start()

    def wait(self, i):
        src, dst, device = self.ends(i)
        rdma(src, dst, self.ss.at[i], self.rs.at[i], device).wait_recv()

    def wait_sends(self):
        for i in range(13):
            src, dst, device = self.ends(i)
            rdma(src, dst, self.ss.at[i], self.rs.at[i], device).wait_send()

    def s1(self):
        self.wait(0)
        for i in range(4):
            self.sums[i] = add(self.part[self.me.k, i], self.fromsib[i]).astype(BF16)
        self.send(1)
        self.send(2)

    def s2(self):
        me, h = self.me, self.half
        self.wait(1)
        self.sums[me.xright, 0:h] = add(self.sums[me.xright, 0:h], self.h1[0]).astype(BF16)
        self.send(3)
        self.wait(2)
        self.sums[me.xleft, h : 2 * h] = add(self.sums[me.xleft, h : 2 * h], self.h1[1]).astype(BF16)
        self.send(4)

    def s3(self):
        me = self.me
        self.wait(3)
        self.wait(4)
        total = add(self.sums[me.x], self.h2[0], self.h2[1])
        for q in range(4):
            for h in range(2):
                self.b[q, h] = self.split(total, q, h).astype(BF16)
        self.send(5)
        self.send(6)

    def s4(self):
        me = self.me
        self.wait(5)
        self.b[me.zright, 0] = add(self.b[me.zright, 0], self.z1[0]).astype(BF16)
        self.send(7)
        self.wait(6)
        self.b[me.zleft, 1] = add(self.b[me.zleft, 1], self.z1[1]).astype(BF16)
        self.send(8)

    def s5(self):
        me = self.me
        self.wait(7)
        self.wait(8)
        self.g[me.z] = add(self.b[me.z], self.z2[0], self.z2[1]).astype(BF16)
        self.send(9)
        self.send(10)

    def s6(self):
        self.wait(9)
        self.send(11)
        self.wait(10)
        self.send(12)

    def s7(self):
        self.wait(11)
        self.wait(12)


class Sum:
    def __init__(self, me, part, s1, r1, s2, r2, out, ss, rs):
        self.me, self.part, self.s1, self.r1, self.s2, self.r2, self.out = me, part, s1, r1, s2, r2, out
        self.ss, self.rs = ss, rs

    def copy(self, step, j):
        me = self.me
        src, dst, device = {
            0: lambda: (self.s1.at[flip(me.y, j + 1)], self.r1.at[j], me.ys[j]),
            1: lambda: (self.s2, self.r2.at[j], me.zs[j]),
            2: lambda: (self.out.at[me.y], self.out.at[me.y], me.ys[j]),
        }[step]()
        return rdma(src, dst, self.ss.at[step * 3 + j], self.rs.at[step * 3 + j], device)

    def t1(self):
        for q in range(4):
            self.s1[q] = self.part[q].astype(BF16)
        for j in range(3):
            self.copy(0, j).start()

    def t2(self):
        for j in range(3):
            self.copy(0, j).wait_recv()
        total = add(self.part[self.me.y], *[self.r1[j] for j in range(3)])
        self.part[self.me.y] = total
        self.s2[...] = total.astype(BF16)
        for j in range(3):
            self.copy(1, j).start()

    def t3(self):
        for j in range(3):
            self.copy(1, j).wait_recv()
        self.out[self.me.y] = add(self.part[self.me.y], *[self.r2[j] for j in range(3)]).astype(BF16)
        for j in range(3):
            self.copy(2, j).start()

    def t4(self):
        for j in range(3):
            self.copy(2, j).wait_recv()

    def wait_sends(self):
        for step in range(3):
            for j in range(3):
                self.copy(step, j).wait_send()


def kernel(
    feat_ref, cot_ref, w_ref, left_ref, act_ref, fg_ref, bg_ref, lgr_ref, rg_ref,
    xall, wg, lgat, wz, xt, lowt, part, t_s1, t_r1, t_s2, t_r2, lowq, pre, gp, dfeat, ds_, dr_,
    m_p, m_sr, m_a, m_h1, m_h2, m_b, m_z1, m_z2, m_g,
    l_p, l_sr, l_a, l_h1, l_h2, l_b, l_z1, l_z2, l_g,
    ga_s, ga_r, rd_s, rd_r, su_s, su_r, x_s, x_r, d_s, d_r,
):
    me = Place()
    barrier = pltpu.get_barrier_semaphore()
    for device in me.all:
        pl.semaphore_signal(barrier, inc=1, device_id=device, device_id_type=pl.DeviceIdType.MESH)

    for p in range(PAIRS):
        xall[0, p] = feat_ref[:, p * LANES : (p + 1) * LANES]
    lgat[me.x, me.k] = left_ref[...]
    for c in range(PAIRS):
        wg[c, me.x, me.k] = w_ref[c]
    pl.semaphore_wait(barrier, len(me.all))

    gather_left = Gather(me, left_ref, lgat, ga_s.at[4], ga_r.at[4], LROWS)

    def gather(c):
        return Gather(me, w_ref.at[c], wg.at[c], ga_s.at[c], ga_r.at[c], ROWS)

    def level(j):
        return rdma(xall.at[0], xall.at[j + 1], x_s.at[j], x_r.at[j], me.levels[j])

    def term(j, c):
        return rdma(ds_.at[j, c], dr_.at[j, c], d_s.at[j, c], d_r.at[j, c], me.levels[j])

    def total(a):
        return Sum(
            me, part.at[a], t_s1.at[a], t_r1.at[a], t_s2.at[a], t_r2.at[a], lowq.at[a], su_s.at[a], su_r.at[a]
        )

    def split_main(v, q, h):
        return v[48 * q : 48 * q + 48, LANES * h : LANES * (h + 1)]

    def split_left(v, q, h):
        return v[16 * h : 16 * h + 16, LANES * q : LANES * (q + 1)]

    def reduce_main(c):
        bufs = [r.at[c] for r in (m_p, m_sr, m_a, m_h1, m_h2, m_b, m_z1, m_z2, m_g)]
        return Reduce(me, bufs, rd_s.at[c], rd_r.at[c], ROWS // 2, split_main)

    reduce_left = Reduce(
        me, (l_p, l_sr, l_a, l_h1, l_h2, l_b, l_z1, l_z2, l_g), rd_s.at[4], rd_r.at[4], LROWS // 2, split_left
    )

    gather_left.first()
    for j in range(4):
        level(j).start()
    for c in range(PAIRS):
        gather(c).first()

    def clear(i, carry):
        wz[lax.div(i, 9), pl.ds(lax.rem(i, 9) * 128, 128), :] = jnp.zeros((128, NH), BF16)
        return carry

    lax.fori_loop(0, PAIRS * 9, clear, 0)
    dfeat[...] = jnp.zeros_like(dfeat)
    part[1] = jnp.zeros((4, 64, 256), F32)

    gather_left.second()
    gather_left.third()
    gather_left.last()
    features = jnp.concatenate([xall[0, p] for p in range(PAIRS)], axis=1)
    low_part = lax.dot_general(features, lgat[...].reshape(256, 512), NT, preferred_element_type=F32)
    part[0] = low_part.reshape(4, 64, 256)
    total(0).t1()
    gather(0).second()
    gather(1).second()
    total(0).t2()
    gather(2).second()
    gather(3).second()
    gather(0).third()
    total(0).t3()
    for c in range(1, PAIRS):
        gather(c).third()
    for j in range(4):
        level(j).wait_recv()

    def turn(c, carry):
        for j in range(7):
            if j == 0:
                tile = xall[0, c]
            elif j == 1:
                tile = xall[0, flip(c, 1)]
            elif j == 2:
                tile = xall[0, flip(c, 2)]
            else:
                tile = xall[j - 2, c]
            turned = tile.T
            if j == 0:
                for gi in range(2):
                    xt[2 * c + gi, 0:64, :] = turned[64 * gi : 64 * gi + 64]
                    xt[2 * c + gi, 64:128, :] = turned[64 * (1 - gi) : 64 * (1 - gi) + 64]
            else:
                for gi in range(2):
                    xt[2 * c + gi, 64 * (j + 1) : 64 * (j + 2), :] = turned[64 * gi : 64 * gi + 64]
        return carry

    lax.fori_loop(0, PAIRS, turn, 0)
    total(0).t4()
    lowt[...] = lowq[0].reshape(256, 256).T

    def compute(c):
        gather(c).last()
        for gi in range(2):
            block = wg[c, :, :, 64 * gi : 64 * gi + 64, :].astype(F32).reshape(8, 64, COLS)
            for t in range(8):
                row = gi * 64 if t == 0 else (1 - gi) * 64 if t == 1 else (t - 1) * LANES + gi * 64
                rows = block[:, 8 * t : 8 * t + 8, :].reshape(64, COLS).astype(BF16)
                wz[c, row : row + 64, COLS * gi : COLS * (gi + 1)] = rows
            right = wg[c, :, :, 128 + 32 * gi : 160 + 32 * gi, :].reshape(256, COLS)
            wz[c, 896:1152, COLS * gi : COLS * (gi + 1)] = right
        tiles = [xall[0, c], xall[0, flip(c, 1)], xall[0, flip(c, 2)]] + [xall[j, c] for j in range(1, 5)]
        xcat = jnp.concatenate(tiles + [lowq[0].reshape(256, 256)], axis=1)
        pre[...] = jnp.dot(xcat, wz[c], preferred_element_type=F32)

        def gelu(i, carry):
            rows = pl.ds(i * 32, 32)
            cols = pl.ds(pl.multiple_of(c * NH, NH), NH)
            v = pre[rows, :]
            th = jnp.tanh(GELU_A * (v + GELU_B * (v * v * v)))
            half = 0.5 * (1.0 + th)
            act_ref[rows, cols] = (v * half).astype(BF16)
            slope = half + 0.5 * v * (1.0 - th * th) * (GELU_A * (1.0 + 3.0 * GELU_B * (v * v)))
            gp[rows, :] = (cot_ref[rows, cols].astype(F32) * slope).astype(BF16)
            return carry

        lax.fori_loop(0, 8, gelu, 0)

        for gi in range(2):
            g = gp[:, COLS * gi : COLS * (gi + 1)]
            grad = jnp.dot(xt[2 * c + gi], g, preferred_element_type=F32).reshape(4, 2, 8, 8, COLS)
            for tp in range(4):
                for f in range(8):
                    rows = jnp.concatenate([grad[tp, 0, f], grad[tp, 1, f]], axis=0).astype(BF16)
                    m_p[c, f % 2, f // 2, 64 * gi + 16 * tp : 64 * gi + 16 * tp + 16, :] = rows
            grad = jnp.dot(lowt[...], g, preferred_element_type=F32).astype(BF16)
            for f in range(8):
                m_p[c, f % 2, f // 2, 128 + 32 * gi : 160 + 32 * gi, :] = grad[32 * f : 32 * f + 32]
        reduce_main(c).send(0)

        def back(first, last):
            return lax.dot_general(gp[...], wz[c, first:last, :], NT, preferred_element_type=F32)

        far = back(384, 640)
        for j in range(2):
            ds_[j, c] = far[:, LANES * j : LANES * (j + 1)].astype(BF16)
            term(j, c).start()
        far = back(640, 896)
        for j in range(2):
            ds_[j + 2, c] = far[:, LANES * j : LANES * (j + 1)].astype(BF16)
            term(j + 2, c).start()
        near = back(0, 256)
        dfeat[c] += near[:, :LANES]
        dfeat[flip(c, 1)] += near[:, LANES:]
        dfeat[flip(c, 2)] += back(256, 384)
        part[1] += back(896, 1152).reshape(4, 64, 256)

    def write_main(c):
        for_q = [jnp.concatenate([m_g[c, q, 0].astype(F32), m_g[c, q, 1].astype(F32)], axis=1) for q in range(4)]
        rows = jnp.concatenate(for_q, axis=0)
        for gi in range(2):
            for t in range(8):
                first = 64 * gi + 8 * t
                bg_ref[t, 2 * c + gi] = rows[first : first + 8]
            cols = pl.ds(pl.multiple_of((2 * c + gi) * COLS, COLS), COLS)
            rg_ref[:, cols] = rows[128 + 32 * gi : 160 + 32 * gi]

    def left_start():
        glow = lowq[1].reshape(256, 256)
        mine = jnp.concatenate([xall[0, p] for p in range(PAIRS)], axis=1)
        grad = jnp.dot(glow.T, mine, preferred_element_type=F32).astype(BF16)
        for f in range(8):
            l_p[f % 2, f // 2] = grad[LROWS * f : LROWS * (f + 1)]
        reduce_left.send(0)

    def feature_grad():
        for j in range(4):
            for c in range(PAIRS):
                term(j, c).wait_recv()
        glow = lowq[1].reshape(256, 256)
        low = jnp.dot(glow, lgat[...].reshape(256, 512), preferred_element_type=F32)
        for c in range(PAIRS):
            cols = slice(LANES * c, LANES * (c + 1))
            fg_ref[:, cols] = add(low[:, cols], dfeat[c], *[dr_[j, c] for j in range(4)]).astype(BF16)

    def write_left():
        for q in range(4):
            for h in range(2):
                lgr_ref[16 * h : 16 * h + 16, LANES * q : LANES * (q + 1)] = l_g[q, h].astype(F32)

    left_at = 6

    def tick(i, carry):
        for step in range(7, 0, -1):

            @pl.when(i == left_at + step)
            def _(step=step):
                getattr(reduce_left, f"s{step}")()
                if step == 7:
                    write_left()

        @pl.when(i == 4)
        def _():
            total(1).t2()

        @pl.when(i == 5)
        def _():
            total(1).t3()

        @pl.when(i == 6)
        def _():
            total(1).t4()
            left_start()

        for step in range(7, 0, -1):
            c = i - step

            @pl.when((c >= 0) & (c < PAIRS))
            def _(step=step, c=c):
                getattr(reduce_main(c), f"s{step}")()
                if step == 7:
                    write_main(c)

        @pl.when(i < PAIRS)
        def _():
            compute(i)

        @pl.when(i == PAIRS - 1)
        def _():
            total(1).t1()

        @pl.when(i == 9)
        def _():
            feature_grad()

        return carry

    lax.fori_loop(0, left_at + 8, tick, 0)

    gather_left.wait_sends()
    reduce_left.wait_sends()
    for a in range(2):
        total(a).wait_sends()
    for j in range(4):
        level(j).wait_send()

    def drain(c, carry):
        gather(c).wait_sends()
        reduce_main(c).wait_sends()
        for j in range(4):
            term(j, c).wait_send()
        return carry

    lax.fori_loop(0, PAIRS, drain, 0)


def local(features, cotangent, butterfly, left_factor, right_factor):
    rows = butterfly.transpose(1, 0, 2, 3).reshape(PAIRS, 128, COLS)
    right = right_factor.reshape(32, 8, COLS).transpose(1, 0, 2).reshape(PAIRS, 64, COLS)
    shard = jnp.concatenate([rows, right], axis=1)
    vmem = pltpu.VMEM
    dma = pltpu.SemaphoreType.DMA
    scratch = [
        vmem((5, 4, TOK, LANES), BF16),
        vmem((4, 4, 2, ROWS, COLS), BF16),
        vmem((4, 2, LROWS, LCOLS), BF16),
        vmem((4, KZ, NH), BF16),
        vmem((8, 512, TOK), BF16),
        vmem((256, 256), BF16),
        vmem((2, 4, 64, 256), F32),
        vmem((2, 4, 64, 256), BF16),
        vmem((2, 3, 64, 256), BF16),
        vmem((2, 64, 256), BF16),
        vmem((2, 3, 64, 256), BF16),
        vmem((2, 4, 64, 256), BF16),
        vmem((TOK, NH), F32),
        vmem((TOK, NH), BF16),
        vmem((4, TOK, LANES), F32),
        vmem((4, 4, TOK, LANES), BF16),
        vmem((4, 4, TOK, LANES), BF16),
    ]
    for lead, r, c, quarter in (((4,), ROWS, COLS, 48), ((), LROWS, LCOLS, 16)):
        scratch += [
            vmem(lead + (2, 4, r, c), BF16),
            vmem(lead + (4, r, c), BF16),
            vmem(lead + (4, r, c), BF16),
            vmem(lead + (2, r // 2, c), BF16),
            vmem(lead + (2, r, c), BF16),
            vmem(lead + (4, 2, quarter, LANES), BF16),
            vmem(lead + (2, quarter, LANES), BF16),
            vmem(lead + (2, 2, quarter, LANES), BF16),
            vmem(lead + (4, 2, quarter, LANES), BF16),
        ]
    for shape in ((5, 8), (5, 13), (2, 9), (4,), (4, 4)):
        scratch += [dma(shape), dma(shape)]
    act, fg, bg, lg, rg = pl.pallas_call(
        kernel,
        out_shape=[
            jax.ShapeDtypeStruct((TOK, 2048), BF16),
            jax.ShapeDtypeStruct((TOK, 512), BF16),
            jax.ShapeDtypeStruct((8, 8, 8, 256), F32),
            jax.ShapeDtypeStruct((LROWS, LCOLS), F32),
            jax.ShapeDtypeStruct((32, 2048), F32),
        ],
        in_specs=[pl.BlockSpec(memory_space=vmem)] * 4,
        out_specs=[pl.BlockSpec(memory_space=vmem)] * 5,
        scratch_shapes=scratch,
        compiler_params=pltpu.CompilerParams(
            collective_id=0, has_side_effects=True, vmem_limit_bytes=48 * 1024 * 1024
        ),
        cost_estimate=pl.CostEstimate(flops=4_000_000_000, bytes_accessed=6_000_000, transcendentals=600_000),
    )(features, cotangent, shard, left_factor.T)
    return act, fg, bg, lg.T, rg


def solution(mesh):
    specs = (
        P(("dp", "fsdp"), "tensor"),
        P(("dp", "fsdp"), "tensor"),
        P(None, "tensor", "fsdp", None),
        P("tensor", "fsdp"),
        P("fsdp", "tensor"),
    )
    return jax.shard_map(local, mesh=mesh, in_specs=specs, out_specs=specs, check_vma=False)
```
